32 devices in a mesh: groups: 2 (over y), rows: 4 (over z), cols: 4 (over x, core).
Axes of the slice: x: 2, y: 2, z: 4, core: 2. Of those that a mesh axis runs over, the one named last changes fastest.
Arguments:
- queries: bfloat16 [4096, 1024], P(('groups', 'rows', 'cols')), parts along dimension 0, may hold values from -4.25 to 4.25
- keys: bfloat16 [4096, 128], P(('groups', 'rows', 'cols')), parts along dimension 0, may hold values from -4.25 to 4.25
- values: bfloat16 [4096, 128], P(('groups', 'rows', 'cols')), parts along dimension 0, may hold values from -6 to 6
- positions: int32 [4096], P(('groups', 'rows', 'cols')), parts along dimension 0, may hold values from 0 to 2047, as said below
Outputs:
- attended: bfloat16 [4096, 1024], P(('groups', 'rows', 'cols')), parts along dimension 0
The draws below stay inside these ranges and needn't reach their ends.
There are 2 independent parts, one for each index of `groups`. The reference program is written for one: setup_inputs(seed, part) draws one part's arguments, and reference() takes and returns one part's arrays. A program takes and returns all parts, laid end to end along the dimension named above; each array names one. Nothing has to cross between parts.
Inputs may be any that keep to these rules, and one draw needn't show every extreme that they name: `positions`: a permutation of 0 to 2047.
All inputs are finite; a program needn't handle non-finite values.
Results may differ from the reference program's by a relative error of at most 0.015.
Values may be sent and summed in bfloat16 or wider, within the bound.
A program may use at most 64 MiB of HBM per device.

```python
import math
import jax
import jax.numpy as jnp
from jax import lax

HEADS = 8
HEAD_DIM = 128
TOKENS = 2048


def shared_order(key):
    order = jax.random.permutation(jax.random.fold_in(key, 11), TOKENS).astype(jnp.int32)
    return order


def draw_positions(key, part):
    return shared_order(key)


def draw_keys(key, part):
    base = jnp.clip(jax.random.normal(jax.random.fold_in(key, 12), (TOKENS, HEAD_DIM), jnp.float32), -4.0, 4.0)
    return base.astype(jnp.bfloat16)


def draw_queries(key, part):
    base = jnp.clip(jax.random.normal(jax.random.fold_in(key, 14), (TOKENS, HEADS * HEAD_DIM), jnp.float32), -4.0, 4.0)
    return base.astype(jnp.bfloat16)


def block_scale(key, extent, shards, smallest, high):
    gain = 1.0
    for dim, blocks in shards:
        draws = jax.random.uniform(jax.random.fold_in(jax.random.fold_in(key, 6), dim), (blocks,), jnp.float32, smallest / len(shards), high / len(shards))
        gain = gain * jnp.repeat(jnp.exp(draws), extent[dim] // blocks).reshape((-1,) + (1,) * (len(extent) - 1 - dim))
    return gain


def scatter_about(stream_key, dims, width, reach, pieces=(), held_as=jnp.bfloat16):
    drawn = width * jax.random.normal(stream_key, dims, jnp.float32)
    if pieces:
        drawn = drawn * block_scale(stream_key, dims, pieces, -0.22, 0.18)
    return jnp.clip(drawn, -reach, reach).astype(held_as)


def setup_inputs(seed: int = 0, part: int = 0) -> dict:
    key_of = jax.random.split(jax.random.key(seed), 5)
    part_splits = jax.random.split(jax.random.fold_in(key_of[4], part), 5)
    return {
        "queries": draw_queries(jax.random.fold_in(jax.random.fold_in(key_of[4], part), 71), part),
        "keys": draw_keys(jax.random.fold_in(jax.random.fold_in(key_of[4], part), 71), part),
        "values": scatter_about(part_splits[2], (TOKENS, HEAD_DIM), 1.0, 6.0, ((0, 16),)),
        "positions": draw_positions(jax.random.fold_in(jax.random.fold_in(key_of[4], part), 71), part),
    }


def reference(queries, keys, values, positions):
    total = queries.shape[0]
    block = math.gcd(total, 256)
    scale = HEAD_DIM ** -0.5
    query_heads = queries.reshape(total // block, block, HEADS, HEAD_DIM)
    query_pos = positions.reshape(total // block, block)
    keys_wide = keys.astype(jnp.float32)
    values_wide = values.astype(jnp.float32)

    def one_block(item):
        query_tile, pos_tile = item
        scores = jnp.einsum("qhd,kd->qhk", query_tile.astype(jnp.float32), keys_wide) * scale
        visible = positions[None, None, :] <= pos_tile[:, None, None]
        row_max = jnp.max(jnp.where(visible, scores, -1e30), axis=2, keepdims=True)
        weights = jnp.where(visible, jnp.exp(scores - row_max), 0.0).astype(jnp.bfloat16)
        wide = weights.astype(jnp.float32)
        denominators = jnp.sum(wide, axis=2)
        numerators = jnp.einsum("qhk,kd->qhd", wide, values_wide)
        result = (numerators / denominators[:, :, None]).astype(jnp.bfloat16)
        return result.reshape(block, HEADS * HEAD_DIM)

    return lax.map(one_block, (query_heads, query_pos)).reshape(total, HEADS * HEAD_DIM)
```

```python
import functools
import math

import jax
import jax.numpy as jnp
from jax import lax
from jax.experimental import pallas as pl
from jax.experimental.pallas import tpu as pltpu
from jax.sharding import PartitionSpec as P

HEADS = 8
HEAD_DIM = 128
NEG = -1e30
EXTRA = 16
HEAD_BLOCK = 2
MESH = pl.DeviceIdType.MESH


def kernel(rows, cols, q_ref, k_ref, v_ref, pos_ref, out_ref, buf, qs, qpos, run_max, acc, send_sem, recv_sem):
    length = k_ref.shape[0]
    pair = 2 if cols % 2 == 0 else 1
    wide = cols // pair
    count = rows * cols
    r, c = lax.axis_index("rows"), lax.axis_index("cols")
    x, core = c // pair, c % pair

    def slot(d, e, f):
        return (d * wide + e) * pair + f

    def row_at(d):
        return {"rows": lax.rem(r + d, rows), "cols": c}

    def wide_at(e):
        return {"rows": r, "cols": lax.rem(x + e, wide) * pair + core}

    def core_at():
        return {"rows": r, "cols": x * pair + (1 - core)}

    partners = [row_at(d) for d in range(1, rows)]
    partners += [wide_at(e) for e in range(1, wide)]
    partners += [core_at()] if pair == 2 else []
    barrier = pltpu.get_barrier_semaphore()
    for device in partners:
        pl.semaphore_signal(barrier, inc=1, device_id=device, device_id_type=MESH)

    position = pos_ref[...]
    buf[0, 0:length, :] = k_ref[...]
    buf[0, length : 2 * length, :] = v_ref[...]
    line = lax.broadcasted_iota(jnp.int32, (EXTRA, length), 0)
    digits = jnp.where(line == 0, position >> 7, jnp.where(line == 1, position & 127, 0))
    buf[0, 2 * length :, :] = digits.astype(jnp.float32).astype(jnp.bfloat16)

    pl.semaphore_wait(barrier, len(partners))

    copies = {}

    def send(source, target, device):
        copy = pltpu.make_async_remote_copy(
            src_ref=buf.at[source],
            dst_ref=buf.at[target],
            send_sem=send_sem.at[target],
            recv_sem=recv_sem.at[target],
            device_id=device,
            device_id_type=MESH,
        )
        copy.start()
        copies[target] = copy

    def to_core(d, e):
        if pair == 2:
            send(slot(d, e, 0), slot(d, e, 1), core_at())

    def spread(d):
        for e in range(1, wide):
            send(slot(d, 0, 0), slot(d, e, 0), wide_at(e))
        to_core(d, 0)

    def take_row(d):
        copies[slot(d, 0, 0)].wait_recv()
        spread(d)

    def take_wide(d):
        for e in range(1, wide):
            copies[slot(d, e, 0)].wait_recv()
            to_core(d, e)

    def take_core(d):
        if pair == 2:
            for e in range(wide):
                copies[slot(d, e, 1)].wait_recv()

    for d in range(1, rows):
        send(0, slot(d, 0, 0), row_at(d))
    spread(0)

    factor = math.log2(math.e) / math.sqrt(HEAD_DIM)
    for h in range(HEADS):
        scaled = q_ref[:, h * HEAD_DIM : (h + 1) * HEAD_DIM].astype(jnp.float32) * factor
        high = scaled.astype(jnp.bfloat16)
        low = (scaled - high.astype(jnp.float32)).astype(jnp.bfloat16)
        qs[h, :, 0:HEAD_DIM] = high
        qs[h, :, HEAD_DIM:] = low
    qpos[...] = jnp.transpose(jnp.broadcast_to(position.astype(jnp.float32), (length, length)))

    def absorb(first, number, fresh):
        block = buf[pl.ds(first, number)]
        key = block[:, 0:length].reshape(number * length, HEAD_DIM)
        value = block[:, length : 2 * length].reshape(number * length, HEAD_DIM)
        digit = block[:, 2 * length :].astype(jnp.float32)
        mine = qpos[...]
        bias = jnp.concatenate(
            [
                jnp.where(digit[i, 0:1] * 128.0 + digit[i, 1:2] <= mine, 0.0, NEG)
                for i in range(number)
            ],
            axis=1,
        )
        key = jnp.concatenate([key, key], axis=1)
        value = jnp.concatenate([value, jnp.ones_like(value)], axis=1)
        size = HEAD_BLOCK * length
        for h in range(0, HEADS, HEAD_BLOCK):
            query = qs[h : h + HEAD_BLOCK].reshape(size, 2 * HEAD_DIM)
            scores = lax.dot_general(
                query, key, (((1,), (1,)), ((), ())), preferred_element_type=jnp.float32
            )
            scores = (scores.reshape(HEAD_BLOCK, length, -1) + bias[None]).reshape(size, -1)
            top = jnp.max(scores, axis=1, keepdims=True)
            span = pl.ds(h * length, size)
            if not fresh:
                before = run_max[span, 0:1]
                top = jnp.maximum(before, top)
            weights = jnp.exp2(scores - top).astype(jnp.bfloat16)
            part = jnp.dot(weights, value, preferred_element_type=jnp.float32)
            if not fresh:
                part = acc[span, :] * jnp.exp2(before - top) + part
            acc[span, :] = part
            run_max[span, :] = jnp.broadcast_to(top, (size, 128))

    group = wide * pair
    if rows <= 4 and group <= 4:
        take_wide(0)
        for d in range(1, rows):
            take_row(d)
            take_wide(d - 1) if d > 1 else None
            if d > 1:
                take_core(d - 2)
                absorb((d - 2) * group, group, d == 2)
        if rows > 1:
            take_wide(rows - 1)
        for d in range(max(rows - 2, 0), rows):
            take_core(d)
            absorb(d * group, group, d == 0)
    else:
        take_wide(0)
        for d in range(1, rows):
            take_row(d)
        for d in range(1, rows):
            take_wide(d)
        for d in range(rows):
            take_core(d)
        number = math.gcd(count, 4)
        absorb(0, number, True)

        @pl.loop(1, count // number)
        def _(step):
            absorb(step * number, number, False)

    for h in range(HEADS):
        span = pl.ds(h * length, length)
        out_ref[:, h * HEAD_DIM : (h + 1) * HEAD_DIM] = (
            acc[span, 0:HEAD_DIM] / acc[span, HEAD_DIM:]
        ).astype(out_ref.dtype)
    for copy in copies.values():
        copy.wait_send()


def shards(rows, cols, queries, keys, values, positions):
    length = keys.shape[0]
    count = rows * cols
    return pl.pallas_call(
        functools.partial(kernel, rows, cols),
        out_shape=jax.ShapeDtypeStruct(queries.shape, jnp.bfloat16),
        in_specs=[pl.BlockSpec(memory_space=pltpu.VMEM)] * 4,
        out_specs=pl.BlockSpec(memory_space=pltpu.VMEM),
        scratch_shapes=[
            pltpu.VMEM((count, 2 * length + EXTRA, HEAD_DIM), jnp.bfloat16),
            pltpu.VMEM((HEADS, length, 2 * HEAD_DIM), jnp.bfloat16),
            pltpu.VMEM((length, length), jnp.float32),
            pltpu.VMEM((HEADS * length, 128), jnp.float32),
            pltpu.VMEM((HEADS * length, 2 * HEAD_DIM), jnp.float32),
            pltpu.SemaphoreType.DMA((count,)),
            pltpu.SemaphoreType.DMA((count,)),
        ],
        compiler_params=pltpu.CompilerParams(
            collective_id=0, has_side_effects=True, vmem_limit_bytes=40 * 1024 * 1024
        ),
    )(queries, keys, values, positions.reshape(1, length))


def solution(mesh):
    rows, cols = mesh.shape["rows"], mesh.shape["cols"]
    whole = P(("groups", "rows", "cols"), None)
    return jax.shard_map(
        functools.partial(shards, rows, cols),
        mesh=mesh,
        in_specs=(whole, whole, whole, P(("groups", "rows", "cols"))),
        out_specs=whole,
        check_vma=False,
    )
```

```python
import functools
import math

import jax
import jax.numpy as jnp
from jax import lax
from jax.experimental import pallas as pl
from jax.experimental.pallas import tpu as pltpu
from jax.sharding import PartitionSpec as P

HEADS = 8
HEAD_DIM = 128
NEG = -1e30
EXTRA = 16
HEAD_BLOCK = 2
MESH = pl.DeviceIdType.MESH


def kernel(rows, cols, q_hbm, k_hbm, v_hbm, pos_hbm, out_ref, q_ref, pos_ref, buf, qs, qpos, run_max, acc, load_sem, send_sem, recv_sem):
    length = k_hbm.shape[0]
    loads = [
        pltpu.make_async_copy(source, target, load_sem.at[i])
        for i, (source, target) in enumerate(
            (
                (pos_hbm, pos_ref),
                (k_hbm, buf.at[0, pl.ds(0, length)]),
                (v_hbm, buf.at[0, pl.ds(length, length)]),
                (q_hbm, q_ref),
            )
        )
    ]
    for load in loads:
        load.start()
    pair = 2 if cols % 2 == 0 else 1
    wide = cols // pair
    count = rows * cols
    r, c = lax.axis_index("rows"), lax.axis_index("cols")
    x, core = c // pair, c % pair

    relay = rows == 4 and wide == 2 and pair == 2
    if relay:
        order = [(0, 0), (1, 0), (3, 0), (0, 1), (2, 0), (1, 1), (3, 1), (2, 1)]
    else:
        order = [(d, e) for d in range(rows) for e in range(wide)]

    def slot(d, e, f):
        return order.index((d, e)) * pair + f

    def row_at(d):
        return {"rows": lax.rem(r + d, rows), "cols": c}

    def wide_at(e):
        return {"rows": r, "cols": lax.rem(x + e, wide) * pair + core}

    def across_at(d):
        return {"rows": lax.rem(r + d, rows), "cols": lax.rem(x + 1, wide) * pair + core}

    def core_at():
        return {"rows": r, "cols": x * pair + (1 - core)}

    near = (1, 3) if relay else range(1, rows)
    partners = [row_at(d) for d in near]
    partners += [across_at(d) for d in near] if relay else []
    partners += [wide_at(e) for e in range(1, wide)]
    partners += [core_at()] if pair == 2 else []
    barrier = pltpu.get_barrier_semaphore()
    for device in partners:
        pl.semaphore_signal(barrier, inc=1, device_id=device, device_id_type=MESH)

    loads[0].wait()
    position = pos_ref[...]
    line = lax.broadcasted_iota(jnp.int32, (EXTRA, length), 0)
    digits = jnp.where(line == 0, position >> 7, jnp.where(line == 1, position & 127, 0))
    buf[0, 2 * length :, :] = digits.astype(jnp.float32).astype(jnp.bfloat16)

    loads[1].wait()
    loads[2].wait()
    pl.semaphore_wait(barrier, len(partners))

    copies = {}

    def send(source, target, device):
        copy = pltpu.make_async_remote_copy(
            src_ref=buf.at[source],
            dst_ref=buf.at[target],
            send_sem=send_sem.at[target],
            recv_sem=recv_sem.at[target],
            device_id=device,
            device_id_type=MESH,
        )
        copy.start()
        copies[target] = copy

    def to_core(d, e):
        if pair == 2:
            send(slot(d, e, 0), slot(d, e, 1), core_at())

    def spread(d):
        for e in range(1, wide):
            send(slot(d, 0, 0), slot(d, e, 0), wide_at(e))
        to_core(d, 0)

    def take_row(d):
        copies[slot(d, 0, 0)].wait_recv()
        spread(d)

    def take_wide(d):
        for e in range(1, wide):
            copies[slot(d, e, 0)].wait_recv()
            to_core(d, e)

    def take_core(d, e):
        if pair == 2:
            copies[slot(d, e, 1)].wait_recv()

    for d in near:
        send(0, slot(d, 0, 0), row_at(d))
    spread(0)

    loads[3].wait()
    factor = math.log2(math.e) / math.sqrt(HEAD_DIM)
    for h in range(HEADS):
        scaled = q_ref[:, h * HEAD_DIM : (h + 1) * HEAD_DIM].astype(jnp.float32) * factor
        high = scaled.astype(jnp.bfloat16)
        low = (scaled - high.astype(jnp.float32)).astype(jnp.bfloat16)
        qs[h, :, 0:HEAD_DIM] = high
        qs[h, :, HEAD_DIM:] = low
    qpos[...] = jnp.transpose(jnp.broadcast_to(position.astype(jnp.float32), (length, length)))

    def absorb(first, number, fresh):
        block = buf[pl.ds(first, number)]
        key = block[:, 0:length].reshape(number * length, HEAD_DIM)
        value = block[:, length : 2 * length].reshape(number * length, HEAD_DIM)
        digit = block[:, 2 * length :].astype(jnp.float32)
        mine = qpos[...]
        bias = jnp.concatenate(
            [
                jnp.where(digit[i, 0:1] * 128.0 + digit[i, 1:2] <= mine, 0.0, NEG)
                for i in range(number)
            ],
            axis=1,
        )
        key = jnp.concatenate([key, key], axis=1)
        value = jnp.concatenate([value, jnp.ones_like(value)], axis=1)
        size = HEAD_BLOCK * length
        for h in range(0, HEADS, HEAD_BLOCK):
            query = qs[h : h + HEAD_BLOCK].reshape(size, 2 * HEAD_DIM)
            scores = lax.dot_general(
                query, key, (((1,), (1,)), ((), ())), preferred_element_type=jnp.float32
            )
            scores = (scores.reshape(HEAD_BLOCK, length, -1) + bias[None]).reshape(size, -1)
            top = jnp.max(scores, axis=1, keepdims=True)
            span = pl.ds(h * length, size)
            if not fresh:
                before = run_max[span, 0:1]
                top = jnp.maximum(before, top)
            weights = jnp.exp2(scores - top).astype(jnp.bfloat16)
            part = jnp.dot(weights, value, preferred_element_type=jnp.float32)
            if not fresh:
                part = acc[span, :] * jnp.exp2(before - top) + part
            acc[span, :] = part
            run_max[span, :] = jnp.broadcast_to(top, (size, 128))

    if relay:
        take_core(0, 0)
        absorb(0, 2, True)
        copies[slot(1, 0, 0)].wait_recv()
        send(slot(1, 0, 0), slot(2, 1, 0), across_at(1))
        send(slot(1, 0, 0), slot(2, 0, 0), row_at(1))
        spread(1)
        take_row(3)
        take_wide(0)
        take_core(1, 0)
        take_core(3, 0)
        absorb(2, 4, False)
        take_core(0, 1)
        absorb(6, 2, False)
        copies[slot(2, 0, 0)].wait_recv()
        to_core(2, 0)
        take_wide(1)
        take_wide(3)
        take_core(2, 0)
        absorb(8, 2, False)
        take_wide(2)
        take_core(1, 1)
        take_core(3, 1)
        absorb(10, 4, False)
        take_core(2, 1)
        absorb(14, 2, False)
    else:
        take_wide(0)
        for d in range(1, rows):
            take_row(d)
        for d in range(1, rows):
            take_wide(d)
        for d in range(rows):
            for e in range(wide):
                take_core(d, e)
        number = math.gcd(count, 4)
        absorb(0, number, True)

        @pl.loop(1, count // number)
        def _(step):
            absorb(step * number, number, False)

    for h in range(HEADS):
        span = pl.ds(h * length, length)
        out_ref[:, h * HEAD_DIM : (h + 1) * HEAD_DIM] = (
            acc[span, 0:HEAD_DIM] / acc[span, HEAD_DIM:]
        ).astype(out_ref.dtype)
    for copy in copies.values():
        copy.wait_send()


def shards(rows, cols, queries, keys, values, positions):
    length = keys.shape[0]
    count = rows * cols
    return pl.pallas_call(
        functools.partial(kernel, rows, cols),
        out_shape=jax.ShapeDtypeStruct(queries.shape, jnp.bfloat16),
        in_specs=[pl.BlockSpec(memory_space=pltpu.HBM)] * 4,
        out_specs=pl.BlockSpec(memory_space=pltpu.VMEM),
        scratch_shapes=[
            pltpu.VMEM(queries.shape, jnp.bfloat16),
            pltpu.VMEM((1, length), jnp.int32),
            pltpu.VMEM((count, 2 * length + EXTRA, HEAD_DIM), jnp.bfloat16),
            pltpu.VMEM((HEADS, length, 2 * HEAD_DIM), jnp.bfloat16),
            pltpu.VMEM((length, length), jnp.float32),
            pltpu.VMEM((HEADS * length, 128), jnp.float32),
            pltpu.VMEM((HEADS * length, 2 * HEAD_DIM), jnp.float32),
            pltpu.SemaphoreType.DMA((4,)),
            pltpu.SemaphoreType.DMA((count,)),
            pltpu.SemaphoreType.DMA((count,)),
        ],
        compiler_params=pltpu.CompilerParams(
            collective_id=0, has_side_effects=True, vmem_limit_bytes=56 * 1024 * 1024
        ),
    )(queries, keys, values, positions.reshape(1, length))


def solution(mesh):
    rows, cols = mesh.shape["rows"], mesh.shape["cols"]
    whole = P(("groups", "rows", "cols"), None)
    return jax.shard_map(
        functools.partial(shards, rows, cols),
        mesh=mesh,
        in_specs=(whole, whole, whole, P(("groups", "rows", "cols"))),
        out_specs=whole,
        check_vma=False,
    )
```

```python
import functools
import math

import jax
import jax.numpy as jnp
from jax import lax
from jax.experimental import pallas as pl
from jax.experimental.pallas import tpu as pltpu
from jax.sharding import PartitionSpec as P

HEADS = 8
HEAD_DIM = 128
NEG = -1e30
EXTRA = 16
HEAD_BLOCK = 2
MESH = pl.DeviceIdType.MESH


def kernel(rows, cols, q_hbm, k_hbm, v_hbm, pos_hbm, out_ref, q_ref, pos_ref, buf, qs, qpos, run_max, acc, load_sem, send_sem, recv_sem):
    length = k_hbm.shape[0]
    loads = [
        pltpu.make_async_copy(source, target, load_sem.at[i])
        for i, (source, target) in enumerate(
            (
                (pos_hbm, pos_ref),
                (k_hbm, buf.at[0, pl.ds(0, length)]),
                (v_hbm, buf.at[0, pl.ds(length, length)]),
                (q_hbm, q_ref),
            )
        )
    ]
    for load in loads:
        load.start()
    pair = 2 if cols % 2 == 0 else 1
    wide = cols // pair
    count = rows * cols
    r, c = lax.axis_index("rows"), lax.axis_index("cols")
    x, core = c // pair, c % pair

    relay = rows == 4 and wide == 2 and pair == 2
    if relay:
        order = [(0, 0), (1, 0), (3, 0), (0, 1), (2, 0), (1, 1), (3, 1), (2, 1)]
    else:
        order = [(d, e) for d in range(rows) for e in range(wide)]

    def slot(d, e, f):
        return order.index((d, e)) * pair + f

    def row_at(d):
        return {"rows": lax.rem(r + d, rows), "cols": c}

    def wide_at(e):
        return {"rows": r, "cols": lax.rem(x + e, wide) * pair + core}

    def across_at(d):
        return {"rows": lax.rem(r + d, rows), "cols": lax.rem(x + 1, wide) * pair + core}

    def core_at():
        return {"rows": r, "cols": x * pair + (1 - core)}

    near = (1, 3) if relay else range(1, rows)
    partners = [row_at(d) for d in near]
    partners += [across_at(d) for d in near] if relay else []
    partners += [wide_at(e) for e in range(1, wide)]
    partners += [core_at()] if pair == 2 else []
    barrier = pltpu.get_barrier_semaphore()
    for device in partners:
        pl.semaphore_signal(barrier, inc=1, device_id=device, device_id_type=MESH)

    loads[0].wait()
    position = pos_ref[...]
    line = lax.broadcasted_iota(jnp.int32, (EXTRA, length), 0)
    digits = jnp.where(line == 0, position >> 7, jnp.where(line == 1, position & 127, 0))
    buf[0, 2 * length :, :] = digits.astype(jnp.float32).astype(jnp.bfloat16)

    loads[1].wait()
    loads[2].wait()
    pl.semaphore_wait(barrier, len(partners))

    copies = {}

    def send(source, target, device):
        copy = pltpu.make_async_remote_copy(
            src_ref=buf.at[source],
            dst_ref=buf.at[target],
            send_sem=send_sem.at[target],
            recv_sem=recv_sem.at[target],
            device_id=device,
            device_id_type=MESH,
        )
        copy.start()
        copies[target] = copy

    def to_core(d, e):
        if pair == 2:
            send(slot(d, e, 0), slot(d, e, 1), core_at())

    def spread(d):
        for e in range(1, wide):
            send(slot(d, 0, 0), slot(d, e, 0), wide_at(e))
        to_core(d, 0)

    def take_row(d):
        copies[slot(d, 0, 0)].wait_recv()
        spread(d)

    def take_wide(d):
        for e in range(1, wide):
            copies[slot(d, e, 0)].wait_recv()
            to_core(d, e)

    def take_core(d, e):
        if pair == 2:
            copies[slot(d, e, 1)].wait_recv()

    for d in near:
        send(0, slot(d, 0, 0), row_at(d))
    spread(0)

    loads[3].wait()
    factor = math.log2(math.e) / math.sqrt(HEAD_DIM)
    for h in range(HEADS):
        scaled = q_ref[:, h * HEAD_DIM : (h + 1) * HEAD_DIM].astype(jnp.float32) * factor
        high = scaled.astype(jnp.bfloat16)
        low = (scaled - high.astype(jnp.float32)).astype(jnp.bfloat16)
        qs[h, :, 0:HEAD_DIM] = high
        qs[h, :, HEAD_DIM:] = low
    qpos[...] = jnp.transpose(jnp.broadcast_to(position.astype(jnp.float32), (length, length)))

    def absorb(first, number, fresh):
        block = buf[pl.ds(first, number)]
        key = block[:, 0:length].reshape(number * length, HEAD_DIM)
        value = block[:, length : 2 * length].reshape(number * length, HEAD_DIM)
        digit = block[:, 2 * length :].astype(jnp.float32)
        mine = qpos[...]
        bias = jnp.concatenate(
            [
                jnp.where(digit[i, 0:1] * 128.0 + digit[i, 1:2] <= mine, 0.0, NEG)
                for i in range(number)
            ],
            axis=1,
        )
        key = jnp.concatenate([key, key], axis=1)
        value = jnp.concatenate([value, jnp.ones_like(value)], axis=1)
        size = HEAD_BLOCK * length
        for h in range(0, HEADS, HEAD_BLOCK):
            query = qs[h : h + HEAD_BLOCK].reshape(size, 2 * HEAD_DIM)
            scores = lax.dot_general(
                query, key, (((1,), (1,)), ((), ())), preferred_element_type=jnp.float32
            )
            scores = (scores.reshape(HEAD_BLOCK, length, -1) + bias[None]).reshape(size, -1)
            top = jnp.max(scores, axis=1, keepdims=True)
            span = pl.ds(h * length, size)
            if not fresh:
                before = run_max[span, 0:1]
                top = jnp.maximum(before, top)
            weights = jnp.exp2(scores - top).astype(jnp.bfloat16)
            part = jnp.dot(weights, value, preferred_element_type=jnp.float32)
            if not fresh:
                part = acc[span, :] * jnp.exp2(before - top) + part
            acc[span, :] = part
            run_max[span, :] = jnp.broadcast_to(top, (size, 128))

    if relay:
        copies[slot(1, 0, 0)].wait_recv()
        send(slot(1, 0, 0), slot(2, 1, 0), across_at(1))
        send(slot(1, 0, 0), slot(2, 0, 0), row_at(1))
        spread(1)
        take_row(3)
        take_wide(0)
        take_core(1, 0)
        take_core(3, 0)
        take_core(0, 0)
        take_core(0, 1)
        absorb(0, 8, True)
        copies[slot(2, 0, 0)].wait_recv()
        to_core(2, 0)
        take_wide(1)
        take_wide(3)
        take_core(2, 0)
        take_wide(2)
        take_core(1, 1)
        take_core(3, 1)
        take_core(2, 1)
        absorb(8, 8, False)
    else:
        take_wide(0)
        for d in range(1, rows):
            take_row(d)
        for d in range(1, rows):
            take_wide(d)
        for d in range(rows):
            for e in range(wide):
                take_core(d, e)
        number = math.gcd(count, 4)
        absorb(0, number, True)

        @pl.loop(1, count // number)
        def _(step):
            absorb(step * number, number, False)

    for h in range(HEADS):
        span = pl.ds(h * length, length)
        out_ref[:, h * HEAD_DIM : (h + 1) * HEAD_DIM] = (
            acc[span, 0:HEAD_DIM] / acc[span, HEAD_DIM:]
        ).astype(out_ref.dtype)
    for copy in copies.values():
        copy.wait_send()


def shards(rows, cols, queries, keys, values, positions):
    length = keys.shape[0]
    count = rows * cols
    return pl.pallas_call(
        functools.partial(kernel, rows, cols),
        out_shape=jax.ShapeDtypeStruct(queries.shape, jnp.bfloat16),
        in_specs=[pl.BlockSpec(memory_space=pltpu.HBM)] * 4,
        out_specs=pl.BlockSpec(memory_space=pltpu.VMEM),
        scratch_shapes=[
            pltpu.VMEM(queries.shape, jnp.bfloat16),
            pltpu.VMEM((1, length), jnp.int32),
            pltpu.VMEM((count, 2 * length + EXTRA, HEAD_DIM), jnp.bfloat16),
            pltpu.VMEM((HEADS, length, 2 * HEAD_DIM), jnp.bfloat16),
            pltpu.VMEM((length, length), jnp.float32),
            pltpu.VMEM((HEADS * length, 128), jnp.float32),
            pltpu.VMEM((HEADS * length, 2 * HEAD_DIM), jnp.float32),
            pltpu.SemaphoreType.DMA((4,)),
            pltpu.SemaphoreType.DMA((count,)),
            pltpu.SemaphoreType.DMA((count,)),
        ],
        compiler_params=pltpu.CompilerParams(
            collective_id=0, has_side_effects=True, vmem_limit_bytes=56 * 1024 * 1024
        ),
    )(queries, keys, values, positions.reshape(1, length))


def solution(mesh):
    rows, cols = mesh.shape["rows"], mesh.shape["cols"]
    whole = P(("groups", "rows", "cols"), None)
    return jax.shard_map(
        functools.partial(shards, rows, cols),
        mesh=mesh,
        in_specs=(whole, whole, whole, P(("groups", "rows", "cols"))),
        out_specs=whole,
        check_vma=False,
    )
```
